512 devices in a mesh: dp: 64 (over x, y, core), tensor: 8 (over z).
Axes of the slice: x: 4, y: 8, z: 8, core: 2. Of those that a mesh axis runs over, the one named last changes fastest.
Arguments:
- activations: bfloat16 [16384, 8192], P('dp', 'tensor'), may hold values from -6 to 6
- out_grad: bfloat16 [16384, 8192], P('dp', 'tensor'), may hold values from -6 to 6
- gate_pre: bfloat16 [16384, 16384], P('dp', 'tensor'), may hold values from -8 to 8
- up_pre: bfloat16 [16384, 16384], P('dp', 'tensor'), may hold values from -6 to 6
- hidden_grad: bfloat16 [16384, 16384], P('dp', 'tensor'), may hold values from -6 to 6
- kept_blocks: int32 [8, 3, 64], P('tensor'), may hold values from 0 to 63, as said below
- kept_counts: int32 [8], P('tensor'), may hold values from 16 to 64, as said below
Outputs:
- kept_grads: float32 [64, 8, 128, 128], P('dp', 'tensor')
The draws below stay inside these ranges and needn't reach their ends.
Inputs may be any that keep to these rules, and one draw needn't show every extreme that they name: kept_blocks[j, 0, k] is the matrix: 0 gate, 1 up (row block over the 64 blocks of the model width, column block over the shard's 16 blocks of hidden units), 2 down (row block over the shard's 16 hidden blocks, column block over the 64 width blocks). The 64 entries of one shard are distinct blocks; entries at k >= kept_counts[j] are valid but not kept. `kept_counts`: counts differ between tensor shards; some shard has exactly 64.
All inputs are finite; a program needn't handle non-finite values.
Results may differ from the reference program's by a relative error of at most 0.0029.
Values may be sent and summed in bfloat16 or wider, within the bound.
A program may use at most 128 MiB of HBM per device.

```python
import jax
import jax.numpy as jnp
from jax import lax

D = 8192
FF = 16384
BLK = 128
TOKENS = 16384
SLOTS = 64
SHARDS = 8
DBLK = 64
FBLK = 16


def draw_kept_blocks(key, part):
    key = jax.random.fold_in(key, 5)
    total = 3 * DBLK * FBLK
    keys = jax.random.split(key, SHARDS)
    picks = jnp.stack([jax.random.permutation(keys[j], total)[:SLOTS] for j in range(SHARDS)])
    matrix = picks // (DBLK * FBLK)
    rest = picks % (DBLK * FBLK)
    wide = rest // FBLK
    narrow = rest % FBLK
    rows = jnp.where(matrix == 2, narrow, wide)
    cols = jnp.where(matrix == 2, wide, narrow)
    return jnp.stack([matrix, rows, cols], axis=1).astype(jnp.int32)


def draw_kept_counts(key, part):
    key = jax.random.fold_in(key, 11)
    first, second = jax.random.split(key)
    order = jax.random.permutation(first, SHARDS)
    counts = jax.random.randint(second, (SHARDS,), SLOTS // 4, SLOTS + 1)
    counts = jnp.where(order == 0, SLOTS, counts)
    return counts.astype(jnp.int32)


def levels(stream_key, shape, cuts, low, high):
    factor_of, own = 1.0, jax.random.fold_in(stream_key, 6)
    for axis_at, parts in cuts:
        heights = jnp.exp(jax.random.uniform(jax.random.fold_in(own, axis_at), (parts,), jnp.float32, low / len(cuts), high / len(cuts)))
        factor_of = factor_of * jnp.repeat(heights, shape[axis_at] // parts).reshape([-1 if axis == axis_at else 1 for axis in range(len(shape))])
    return factor_of


def scatter_about(key, extent, scale, limit, shards=(), held_as=jnp.bfloat16):
    array = jax.random.normal(key, extent, jnp.float32) * scale
    if len(shards) > 0:
        array = levels(key, extent, shards, -0.22, 0.18) * array
    return jnp.clip(array, min=-limit, max=limit).astype(held_as)


def setup_inputs(seed: int = 0) -> dict:
    key_list = jax.random.split(jax.random.key(seed), 8)
    activations = scatter_about(key_list[0], (TOKENS, D), 1.0, 6.0, ((0, 64), (1, 8)))
    out_grad = scatter_about(key_list[1], (TOKENS, D), 1.0, 6.0, ((0, 64), (1, 8)))
    gate_pre = scatter_about(key_list[2], (TOKENS, FF), 1.5, 8.0, ((0, 64), (1, 8)))
    up_pre = scatter_about(key_list[3], (TOKENS, FF), 1.0, 6.0, ((0, 64), (1, 8)))
    hidden_grad = scatter_about(key_list[4], (TOKENS, FF), 1.0, 6.0, ((0, 64), (1, 8)))
    kept_blocks = draw_kept_blocks(jax.random.fold_in(key_list[7], 71), 0)
    kept_counts = draw_kept_counts(jax.random.fold_in(key_list[7], 71), 0)
    return dict(activations=activations, out_grad=out_grad, gate_pre=gate_pre, up_pre=up_pre, hidden_grad=hidden_grad, kept_blocks=kept_blocks, kept_counts=kept_counts)


def swiglu_back(gate_pre, up_pre, hidden_grad):
    gate = gate_pre.astype(jnp.float32)
    upper = up_pre.astype(jnp.float32)
    grad = hidden_grad.astype(jnp.float32)
    sigma = jax.nn.sigmoid(gate)
    active = gate * sigma
    hidden = (active * upper).astype(jnp.bfloat16)
    d_gate = (grad * upper * sigma * (1.0 + gate * (1.0 - sigma))).astype(jnp.bfloat16)
    d_up = (grad * active).astype(jnp.bfloat16)
    return hidden, d_gate, d_up


def reference(activations, out_grad, gate_pre, up_pre, hidden_grad, kept_blocks, kept_counts):
    scale = float(TOKENS) ** -0.5
    ff_dev = FF // SHARDS
    results = []
    for shard in range(SHARDS):
        table = kept_blocks[shard]
        count = kept_counts[shard]

        def one_slot(slot):
            mat = table[0, slot]
            rows = table[1, slot]
            cols = table[2, slot]
            fcol = (shard * ff_dev + jnp.where(mat == 2, rows, cols) * BLK).astype(jnp.int32)
            dcol = (jnp.where(mat == 2, cols, rows) * BLK).astype(jnp.int32)
            xs = lax.dynamic_slice_in_dim(activations, dcol, BLK, 1)
            ys = lax.dynamic_slice_in_dim(out_grad, dcol, BLK, 1)
            gs = lax.dynamic_slice_in_dim(gate_pre, fcol, BLK, 1)
            us = lax.dynamic_slice_in_dim(up_pre, fcol, BLK, 1)
            hs = lax.dynamic_slice_in_dim(hidden_grad, fcol, BLK, 1)
            hidden, d_gate, d_up = swiglu_back(gs, us, hs)
            left = jnp.where(mat == 2, hidden, xs).astype(jnp.float32)
            right = jnp.where(mat == 0, d_gate, jnp.where(mat == 1, d_up, ys)).astype(jnp.float32)
            grad = jnp.dot(left.T, right, preferred_element_type=jnp.float32) * scale
            live = (slot < count).astype(jnp.float32)
            return grad * live

        results.append(lax.map(one_slot, jnp.arange(SLOTS, dtype=jnp.int32)))
    return jnp.stack(results, axis=1)
```

```python
import functools

import jax
import jax.numpy as jnp
from jax import lax
from jax.experimental import pallas as pl
from jax.experimental.pallas import tpu as pltpu
from jax.sharding import PartitionSpec as P

BLK = 128
MESH = pl.DeviceIdType.MESH
ROWS = (32, 32, 32, 32)
GROUP = 4
F32 = jnp.float32
BF16 = jnp.bfloat16


def kernel(dims, x_hbm, dy_hbm, gate_hbm, up_hbm, grad_hbm, table, counts, out_ref, x_in, dy_in, gate_in, up_in, grad_in,
           f_buf, acc, load_sem, ring_send, ring_recv, pair_send, pair_recv, sum_send, sum_recv, *bufs):
    dp_n, z_n, tokens, wide, narrow, slots = dims
    waves = len(ROWS)
    d_buf = bufs[0:waves]
    p_out = bufs[waves:2 * waves]
    p_own = bufs[2 * waves:3 * waves]
    p_in = bufs[3 * waves:4 * waves]
    s_buf = bufs[4 * waves:5 * waves]
    r_buf = bufs[5 * waves:6 * waves]
    chips = dp_n // 2
    half = slots // 2
    xb = wide // BLK
    fb = narrow // BLK

    dp = lax.axis_index("dp")
    z = lax.axis_index("tensor")
    core = lax.rem(dp, 2)
    chip = lax.div(dp, 2)
    sibling = dp + 1 - 2 * core
    right, left = lax.rem(z + 1, z_n), lax.rem(z + z_n - 1, z_n)

    loads = [
        pltpu.make_async_copy(src, dst, load_sem.at[i])
        for i, (src, dst) in enumerate(
            ((x_hbm, x_in), (dy_hbm, dy_in), (gate_hbm, gate_in), (up_hbm, up_in), (grad_hbm, grad_in)))
    ]
    for load in loads:
        load.start()

    barrier = pltpu.get_barrier_semaphore()
    for to in (left, right):
        pl.semaphore_signal(barrier, inc=1, device_id=(dp, to), device_id_type=MESH)
    pl.semaphore_signal(barrier, inc=1, device_id=(sibling, z), device_id_type=MESH)

    def greet(o, _):
        pl.semaphore_signal(barrier, inc=1, device_id=(lax.rem(chip + o, chips) * 2 + core, z), device_id_type=MESH)
        return 0

    lax.fori_loop(1, chips, greet, 0)

    starts = [sum(ROWS[:w]) for w in range(waves)]

    def turn(src, base):
        def body(b, _):
            t = src[:, pl.ds(pl.multiple_of(b * BLK, BLK), BLK)].T
            for w in range(waves):
                d_buf[w][0, base + b] = t[starts[w]:starts[w] + ROWS[w]]
            return 0

        lax.fori_loop(0, xb, body, 0)

    def message(w, way, step, part):
        src = (step - 1) if way == 0 else (z_n - (step - 1)) % z_n
        dst = step if way == 0 else z_n - step
        cut = pl.ds(part * xb, xb)
        return pltpu.make_async_remote_copy(
            src_ref=d_buf[w].at[src, cut],
            dst_ref=d_buf[w].at[dst, cut],
            send_sem=ring_send.at[w, way, step - 1, part],
            recv_sem=ring_recv.at[w, way, step - 1, part],
            device_id=(dp, right if way == 0 else left),
            device_id_type=MESH,
        )

    sent = []

    def go(w, way, step, part):
        m = message(w, way, step, part)
        m.start()
        sent.append(m)

    loads[0].wait()
    turn(x_in, 0)
    pl.semaphore_wait(barrier, 3 + chips - 1)
    go(0, 0, 1, 0)
    go(0, 1, 1, 0)
    loads[1].wait()
    turn(dy_in, xb)
    go(0, 0, 1, 1)
    go(0, 1, 1, 1)

    for load in loads[2:]:
        load.wait()

    def back(f, _):
        cols = pl.ds(pl.multiple_of(f * BLK, BLK), BLK)
        g = gate_in[:, cols].astype(F32)
        u = up_in[:, cols].astype(F32)
        d = grad_in[:, cols].astype(F32)
        s = 1.0 / (1.0 + jnp.exp(-g))
        active = g * s
        f_buf[f] = (d * u * s * (1.0 + g * (1.0 - s))).astype(BF16)
        f_buf[fb + f] = (d * active).astype(BF16)
        f_buf[2 * fb + f] = (active * u).astype(BF16)
        return 0

    lax.fori_loop(0, fb, back, 0)

    def products(w, dst, parity, first, last):
        def body(i, _):
            for j in range(GROUP):
                n = i * GROUP + j
                k = 2 * n + parity
                m, r, c = table[0, 0, k], table[0, 1, k], table[0, 2, k]
                down = m == 2
                d = jnp.where(down, c, r)
                f = jnp.where(down, r, c)
                off = lax.rem(z + z_n - lax.div(d, xb), z_n)
                b = lax.rem(d, xb) + jnp.where(down, xb, 0)
                dst[n] = jnp.dot(d_buf[w][off, b], f_buf[m * fb + f], preferred_element_type=F32)
            return 0

        lax.fori_loop(first, last, body, 0)

    def pair(w):
        return pltpu.make_async_remote_copy(
            src_ref=p_out[w], dst_ref=p_in[w], send_sem=pair_send.at[w], recv_sem=pair_recv.at[w],
            device_id=(sibling, z), device_id_type=MESH)

    def spread(w):
        pair(w).wait_recv()

        def add(n, _):
            s_buf[w][n] = (p_own[w][n] + p_in[w][n]).astype(BF16)
            return 0

        lax.fori_loop(0, chips, add, 0)

        def send(o, _):
            to = lax.rem(chip + o, chips)
            pltpu.make_async_remote_copy(
                src_ref=s_buf[w].at[to], dst_ref=r_buf[w].at[o - 1], send_sem=sum_send.at[w], recv_sem=sum_recv.at[w],
                device_id=(to * 2 + core, z), device_id_type=MESH).start()
            return 0

        lax.fori_loop(1, chips, send, 0)

    def all_sums(w):
        return pltpu.make_async_remote_copy(
            src_ref=s_buf[w].at[pl.ds(0, chips - 1)], dst_ref=r_buf[w], send_sem=sum_send.at[w], recv_sem=sum_recv.at[w],
            device_id=(sibling, z), device_id_type=MESH)

    def collect(w):
        all_sums(w).wait_recv()
        total = p_own[w][chip] + p_in[w][chip]
        for o in range(chips - 1):
            total = total + r_buf[w][o].astype(F32)
        acc[pl.ds(starts[w], ROWS[w])] = total

    steps = half // GROUP
    cuts = [0, (steps + 2) // 3, (2 * steps + 2) // 3, steps]

    def work(w, event):
        if event < 3:
            products(w, p_out[w], 1 - core, cuts[event], cuts[event + 1])
            if event == 2:
                pair(w).start()
        else:
            products(w, p_own[w], core, cuts[event - 3], cuts[event - 2])

    def arrived(w, way, step, part):
        message(w, way, step, part).wait_recv()

    for w in range(waves):
        for event in range(6):
            step, part = event // 2 + 1, event % 2
            for way in (0, 1):
                arrived(w, way, step, part)
                if step < 3:
                    go(w, way, step + 1, part)
            if event == 4:
                go(w, 0, 4, 0)
                if w + 1 < waves:
                    go(w + 1, 1, 1, 0)
            if event == 5:
                go(w, 1, 4, 1)
                if w + 1 < waves:
                    go(w + 1, 0, 1, 0)
                    go(w + 1, 0, 1, 1)
                    go(w + 1, 1, 1, 1)
            if w >= 1:
                if event == 0:
                    arrived(w - 1, 0, 4, 0)
                    arrived(w - 1, 1, 4, 1)
                work(w - 1, event)
            if w >= 2:
                if event == 0:
                    spread(w - 2)
                if event == 5:
                    collect(w - 2)
    last = waves - 1
    if waves >= 2:
        spread(last - 1)
    arrived(last, 0, 4, 0)
    arrived(last, 1, 4, 1)
    for event in range(6):
        work(last, event)
    spread(last)
    if waves >= 2:
        collect(last - 1)
    collect(last)

    value = acc[...]
    m = table[0, 0, dp]
    value = jnp.where(m == 2, value.T, value)
    scale = float(tokens * dp_n) ** (-0.5)
    live = (dp < counts[0]).astype(F32)
    out_ref[0, 0] = value * scale * live

    for m in sent:
        m.wait_send()
    for w in range(waves):
        pair(w).wait_send()
        all_sums(w).wait_send()


def solution(mesh):
    dp_n, z_n = mesh.shape["dp"], mesh.shape["tensor"]

    def per_device(activations, out_grad, gate_pre, up_pre, hidden_grad, kept_blocks, kept_counts):
        tokens, wide = activations.shape
        narrow = gate_pre.shape[1]
        slots = kept_blocks.shape[2]
        chips, half = dp_n // 2, slots // 2
        xb, fb = wide // BLK, narrow // BLK
        waves = len(ROWS)
        vmem = pltpu.VMEM
        dma = pltpu.SemaphoreType.DMA
        scratch = [
            vmem((tokens, wide), BF16),
            vmem((tokens, wide), BF16),
            vmem((tokens, narrow), BF16),
            vmem((tokens, narrow), BF16),
            vmem((tokens, narrow), BF16),
            vmem((3 * fb, tokens, BLK), BF16),
            vmem((BLK, BLK), F32),
            dma((5,)),
            dma((waves, 2, 4, 2)),
            dma((waves, 2, 4, 2)),
            dma((waves,)),
            dma((waves,)),
            dma((waves,)),
            dma((waves,)),
        ]
        scratch += [vmem((z_n, 2 * xb, r, tokens), BF16) for r in ROWS]
        scratch += [vmem((half, r, BLK), F32) for r in ROWS]
        scratch += [vmem((half, r, BLK), F32) for r in ROWS]
        scratch += [vmem((half, r, BLK), F32) for r in ROWS]
        scratch += [vmem((chips, r, BLK), BF16) for r in ROWS]
        scratch += [vmem((chips - 1, r, BLK), BF16) for r in ROWS]
        hbm = pl.BlockSpec(memory_space=pl.ANY)
        smem = pl.BlockSpec(memory_space=pltpu.SMEM)
        return pl.pallas_call(
            functools.partial(kernel, (dp_n, z_n, tokens, wide, narrow, slots)),
            out_shape=jax.ShapeDtypeStruct((1, 1, BLK, BLK), F32),
            in_specs=[hbm] * 5 + [smem] * 2,
            out_specs=pl.BlockSpec(memory_space=pltpu.VMEM),
            scratch_shapes=scratch,
            compiler_params=pltpu.CompilerParams(
                collective_id=0, has_side_effects=True, vmem_limit_bytes=62 * 1024 * 1024),
        )(activations, out_grad, gate_pre, up_pre, hidden_grad, kept_blocks, kept_counts)

    return jax.shard_map(
        per_device,
        mesh=mesh,
        in_specs=(P("dp", "tensor"),) * 5 + (P("tensor", None, None), P("tensor")),
        out_specs=P("dp", "tensor", None, None),
        check_vma=False,
    )
```

```python
import functools

import jax
import jax.numpy as jnp
from jax import lax
from jax.experimental import pallas as pl
from jax.experimental.pallas import tpu as pltpu
from jax.sharding import PartitionSpec as P

BLK = 128
LANES = 128
MESH = pl.DeviceIdType.MESH
ROWS = (32, 32, 32, 32)
GROUP = 16
PART = 4
LAG = 2
GAP = PART * LAG
SIZES = (32, 34, 36, 38, 41, 64)
TOP = SIZES[-1]
F32 = jnp.float32
BF16 = jnp.bfloat16
I32 = jnp.int32


def column(row):
    return jnp.broadcast_to(row, (LANES, LANES)).T


def plan_kernel(dims, x_hbm, dy_hbm, table, counts, turned, plan, x_in, dy_in, t_buf, mine, lists, load_sem, out_sem,
                send_sem, recv_sem):
    z_n, xb, fb, slots = dims
    per = 2 * xb
    dp = lax.axis_index("dp")
    z = lax.axis_index("tensor")

    loads = [pltpu.make_async_copy(src, dst, load_sem.at[i]) for i, (src, dst) in enumerate(((x_hbm, x_in), (dy_hbm, dy_in)))]
    for load in loads:
        load.start()
    barrier = pltpu.get_barrier_semaphore()
    for o in range(1, z_n):
        pl.semaphore_signal(barrier, inc=1, device_id=(dp, lax.rem(z + o, z_n)), device_id_type=MESH)

    m, r, c = (table[0, i:i + 1, :] for i in range(3))
    wide_at = jnp.where(m == 2, c, r)
    narrow_at = jnp.where(m == 2, r, c)
    shift = xb.bit_length() - 1
    ids = jnp.right_shift(wide_at, shift) * per + jnp.where(m == 2, xb, 0) + jnp.bitwise_and(wide_at, xb - 1)
    at = lax.broadcasted_iota(I32, (1, slots), 1)
    mine[...] = jnp.full_like(mine, -1)
    mine[0:1, 0:slots] = jnp.where(at < counts[0], ids, -1)
    lists[z] = mine[...]
    pl.semaphore_wait(barrier, z_n - 1)
    swaps = []
    for o in range(1, z_n):
        swap = pltpu.make_async_remote_copy(
            src_ref=mine, dst_ref=lists.at[z], send_sem=send_sem.at[o - 1], recv_sem=recv_sem.at[o - 1],
            device_id=(dp, lax.rem(z + o, z_n)), device_id_type=MESH)
        swap.start()
        swaps.append(swap)

    def turn(src, base):
        def body(b, _):
            t_buf[base + b] = src[:, pl.ds(pl.multiple_of(b * BLK, BLK), BLK)].T
            return 0

        lax.fori_loop(0, xb, body, 0)

    loads[0].wait()
    turn(x_in, 0)
    loads[1].wait()
    turn(dy_in, xb)
    out = pltpu.make_async_copy(t_buf, turned, out_sem)
    out.start()

    for o, swap in enumerate(swaps):
        pltpu.make_async_remote_copy(
            src_ref=mine, dst_ref=lists.at[lax.rem(z + z_n - o - 1, z_n)], send_sem=send_sem.at[o], recv_sem=recv_sem.at[o],
            device_id=(dp, lax.rem(z + o + 1, z_n)), device_id_type=MESH).wait_recv()

    sub = lax.broadcasted_iota(I32, (LANES, LANES), 0)
    lane = lax.broadcasted_iota(I32, (LANES, LANES), 1)
    pshift = per.bit_length() - 1
    lane_row = lax.broadcasted_iota(I32, (1, LANES), 1)
    src_row = jnp.right_shift(lane_row, pshift)
    blk_row = jnp.bitwise_and(lane_row, per - 1).astype(F32)

    def hits(cond, value=1.0):
        return jnp.sum(jnp.where(cond, value, 0.0), axis=0, keepdims=True)

    need = [jnp.zeros((1, LANES), F32) for _ in range(z_n)]
    for j in range(z_n):
        listed = jnp.max(jnp.where(column(lists[j][0:1].astype(F32)) == lane.astype(F32), 1.0, 0.0), axis=0, keepdims=True)
        for d in range(z_n):
            need[d] = jnp.where(src_row == (j - d) % z_n, listed, need[d])
    far = z_n // 2
    reach = []
    for way in (0, 1):
        best = jnp.zeros((1, LANES), F32)
        for d in range(1, far):
            best = jnp.maximum(best, d * need[d if way == 0 else z_n - d])
        reach.append(best)
    odd = jnp.bitwise_and(lane_row, 1).astype(F32)
    lead = reach[0] - reach[1] + 0.5 - odd
    reach = [
        jnp.where(lead > 0, jnp.maximum(reach[0], far * need[far]), reach[0]),
        jnp.where(lead > 0, reach[1], jnp.maximum(reach[1], far * need[far])),
    ]

    same = jnp.right_shift(sub, pshift) == jnp.right_shift(lane, pshift)
    longest = jnp.zeros((1, 1), F32)
    places, orders = [], []
    for way in (0, 1):
        reach_col = column(reach[way])
        ahead = jnp.logical_or(reach_col > reach[way], jnp.logical_and(reach_col == reach[way], sub < lane))
        rank = hits(jnp.logical_and(same, ahead))
        number = [None] + [hits(jnp.logical_and(same, reach_col >= d)) for d in range(1, far + 1)]

        def from_back(row, places_back):
            step = per * places_back if way == 0 else LANES - per * places_back
            full = pltpu.roll(jnp.broadcast_to(row, (8, LANES)), step % LANES, 1)
            return full[0:1]

        start = [None, jnp.zeros((1, LANES), F32)]
        for d in range(2, far + 1):
            before = number[d - 1] if d == 2 else from_back(number[d - 1], d - 2)
            lag = start[d - 1] if d == 2 else from_back(start[d - 1], 1)
            start.append(jnp.maximum(start[d - 1] + before, lag + GAP))
        length = start[far] + from_back(number[far], far - 1)
        longest = jnp.maximum(longest, jnp.max(length, axis=1, keepdims=True))

        def of(row, shard):
            return jnp.max(jnp.where(src_row == shard, row, 0.0), axis=1, keepdims=True)

        back = lax.rem(z + (z_n - 1 if way == 0 else 1), z_n)
        away = jnp.bitwise_and(z - src_row + z_n, z_n - 1)
        if way == 1:
            away = jnp.bitwise_and(z_n - away, z_n - 1)
        got, put = rank, rank
        for d in range(2, far + 1):
            got = got + jnp.where(away == d, of(start[d], back), 0.0)
            put = put + jnp.where(away == d - 1, of(start[d], z), 0.0)
        place = jnp.where(away == 0, blk_row, per + TOP * way + got)
        away_f = away.astype(F32)
        put = jnp.where(jnp.logical_and(away_f < far, reach[way] > away_f), put, -1.0)
        orders.append(hits(column(put) == lane.astype(F32), column(place)))
        places.append(place)

    away = jnp.bitwise_and(z - src_row + z_n, z_n - 1)
    opposite = jnp.where(reach[0] == float(far), places[0], places[1])
    place = jnp.where(away < far, places[0], jnp.where(away == far, opposite, places[1]))
    at_slot = hits(sub == mine[0:1], column(place))

    plan[...] = jnp.zeros_like(plan)
    plan[0:1, :] = orders[0].astype(I32)
    plan[1:2, :] = orders[1].astype(I32)
    plan[2:3, :] = at_slot.astype(I32)
    plan[3:4, 0:slots] = m * fb + narrow_at
    plan[4:5, :] = jnp.broadcast_to(longest, (1, LANES)).astype(I32)
    for swap in swaps:
        swap.wait_send()
    out.wait()


def kernel(dims, turned, gate_hbm, up_hbm, grad_hbm, plan, counts, out_ref, gate_in, up_in, grad_in,
           f_buf, acc, load_sem, own_sem, ring_send, ring_recv, pair_send, pair_recv, sum_send, sum_recv, *bufs):
    room, dp_n, z_n, tokens, per, fb, slots = dims
    waves = len(ROWS)
    held = bufs[0:waves]
    stage = bufs[waves:2 * waves]
    came = bufs[2 * waves:3 * waves]
    p_out = bufs[3 * waves:4 * waves]
    p_own = bufs[4 * waves:5 * waves]
    p_in = bufs[5 * waves:6 * waves]
    s_buf = bufs[6 * waves:7 * waves]
    r_buf = bufs[7 * waves:8 * waves]
    chips = dp_n // 2
    half = slots // 2

    dp = lax.axis_index("dp")
    z = lax.axis_index("tensor")
    core = lax.rem(dp, 2)
    chip = lax.div(dp, 2)
    sibling = dp + 1 - 2 * core
    right, left = lax.rem(z + 1, z_n), lax.rem(z + z_n - 1, z_n)
    starts = [sum(ROWS[:w]) for w in range(waves)]

    own = [
        pltpu.make_async_copy(turned.at[:, pl.ds(starts[w], ROWS[w])], held[w].at[pl.ds(0, per)], own_sem.at[w])
        for w in range(waves)
    ]
    for load in own:
        load.start()
    loads = [
        pltpu.make_async_copy(src, dst, load_sem.at[i])
        for i, (src, dst) in enumerate(((gate_hbm, gate_in), (up_hbm, up_in), (grad_hbm, grad_in)))
    ]
    for load in loads:
        load.start()

    barrier = pltpu.get_barrier_semaphore()
    for to in (left, right):
        pl.semaphore_signal(barrier, inc=1, device_id=(dp, to), device_id_type=MESH)
    pl.semaphore_signal(barrier, inc=1, device_id=(sibling, z), device_id_type=MESH)

    def greet(o, _):
        pl.semaphore_signal(barrier, inc=1, device_id=(lax.rem(chip + o, chips) * 2 + core, z), device_id_type=MESH)
        return 0

    lax.fori_loop(1, chips, greet, 0)

    cuts = [(p, min(p + PART, room)) for p in range(0, room, PART)]
    parts = len(cuts)

    def message(w, way, q):
        first, last = cuts[q]
        cut = pl.ds(first, last - first)
        return pltpu.make_async_remote_copy(
            src_ref=stage[w].at[way, cut], dst_ref=came[w].at[way, cut],
            send_sem=ring_send.at[w, way, q], recv_sem=ring_recv.at[w, way, q],
            device_id=(dp, right if way == 0 else left), device_id_type=MESH)

    def fill(w, q):
        def body(p, _):
            for way in (0, 1):
                stage[w][way, p] = held[w][plan[way, p]]
            return 0

        lax.fori_loop(*cuts[q], body, 0)

    def send(w, q):
        fill(w, q)
        for way in (0, 1):
            message(w, way, q).start()

    def take(w, q):
        for way in (0, 1):
            message(w, way, q).wait_recv()

        def body(p, _):
            for way in (0, 1):
                held[w][per + TOP * way + p] = came[w][way, p]
            return 0

        lax.fori_loop(*cuts[q], body, 0)

    def back(f, _):
        cols = pl.ds(pl.multiple_of(f * BLK, BLK), BLK)
        g = gate_in[:, cols].astype(F32)
        u = up_in[:, cols].astype(F32)
        d = grad_in[:, cols].astype(F32)
        s = 1.0 / (1.0 + jnp.exp(-g))
        active = g * s
        f_buf[f] = (d * u * s * (1.0 + g * (1.0 - s))).astype(BF16)
        f_buf[fb + f] = (d * active).astype(BF16)
        f_buf[2 * fb + f] = (active * u).astype(BF16)
        return 0

    def products(w, dst, parity):
        def body(i, _):
            for j in range(GROUP):
                n = i * GROUP + j
                k = 2 * n + parity
                dst[n] = jnp.dot(held[w][plan[2, k]], f_buf[plan[3, k]], preferred_element_type=F32)
            return 0

        lax.fori_loop(0, half // GROUP, body, 0)

    def pair(w):
        return pltpu.make_async_remote_copy(
            src_ref=p_out[w], dst_ref=p_in[w], send_sem=pair_send.at[w], recv_sem=pair_recv.at[w],
            device_id=(sibling, z), device_id_type=MESH)

    def spread(w):
        pair(w).wait_recv()

        def add(n, _):
            s_buf[w][n] = (p_own[w][n] + p_in[w][n]).astype(BF16)
            return 0

        lax.fori_loop(0, chips, add, 0)

        def post(o, _):
            to = lax.rem(chip + o, chips)
            pltpu.make_async_remote_copy(
                src_ref=s_buf[w].at[to], dst_ref=r_buf[w].at[o - 1], send_sem=sum_send.at[w], recv_sem=sum_recv.at[w],
                device_id=(to * 2 + core, z), device_id_type=MESH).start()
            return 0

        lax.fori_loop(1, chips, post, 0)

    def all_sums(w):
        return pltpu.make_async_remote_copy(
            src_ref=s_buf[w].at[pl.ds(0, chips - 1)], dst_ref=r_buf[w], send_sem=sum_send.at[w], recv_sem=sum_recv.at[w],
            device_id=(sibling, z), device_id_type=MESH)

    def collect(w):
        all_sums(w).wait_recv()
        total = p_own[w][chip] + p_in[w][chip]
        for o in range(chips - 1):
            total = total + r_buf[w][o].astype(F32)
        acc[pl.ds(starts[w], ROWS[w])] = total

    order = [(w, q) for w in range(waves) for q in range(parts)]
    for i, (w, q) in enumerate(order):
        if i >= LAG:
            take(*order[i - LAG])
        if q == 0:
            own[w].wait()
        if i == 0:
            fill(0, 0)
            pl.semaphore_wait(barrier, 3 + chips - 1)
            for way in (0, 1):
                message(0, way, 0).start()
        else:
            send(w, q)
        if i == LAG - 1:
            for load in loads:
                load.wait()
            lax.fori_loop(0, fb, back, 0)
        if w >= 1:
            if q == LAG:
                products(w - 1, p_out[w - 1], 1 - core)
                pair(w - 1).start()
            if q == LAG + 1:
                products(w - 1, p_own[w - 1], core)
            if q == LAG + 2:
                spread(w - 1)
        if w >= 2 and q == LAG + 3:
            collect(w - 2)
    for one in order[-LAG:]:
        take(*one)
    end = waves - 1
    products(end, p_out[end], 1 - core)
    pair(end).start()
    products(end, p_own[end], core)
    spread(end)
    if waves >= 2:
        collect(end - 1)
    collect(end)

    value = acc[...]
    down = plan[3, dp] >= 2 * fb
    value = jnp.where(down, value.T, value)
    scale = float(tokens * dp_n) ** (-0.5)
    live = (dp < counts[0]).astype(F32)
    out_ref[0, 0] = value * scale * live

    for w, q in order:
        for way in (0, 1):
            message(w, way, q).wait_send()
    for w in range(waves):
        pair(w).wait_send()
        all_sums(w).wait_send()


def solution(mesh):
    dp_n, z_n = mesh.shape["dp"], mesh.shape["tensor"]
    vmem = pltpu.VMEM
    dma = pltpu.SemaphoreType.DMA
    hbm = pl.BlockSpec(memory_space=pl.ANY)
    smem = pl.BlockSpec(memory_space=pltpu.SMEM)
    whole = pl.BlockSpec(memory_space=pltpu.VMEM)

    def params(number):
        return pltpu.CompilerParams(collective_id=number, has_side_effects=True, vmem_limit_bytes=62 * 1024 * 1024)

    def per_device(activations, out_grad, gate_pre, up_pre, hidden_grad, kept_blocks, kept_counts):
        tokens, wide = activations.shape
        narrow = gate_pre.shape[1]
        slots = kept_blocks.shape[2]
        chips, half = dp_n // 2, slots // 2
        xb, fb = wide // BLK, narrow // BLK
        per = 2 * xb
        waves = len(ROWS)
        turned, plan = pl.pallas_call(
            functools.partial(plan_kernel, (z_n, xb, fb, slots)),
            out_shape=(jax.ShapeDtypeStruct((per, BLK, tokens), BF16), jax.ShapeDtypeStruct((8, LANES), I32)),
            in_specs=[hbm, hbm, whole, smem],
            out_specs=(hbm, whole),
            scratch_shapes=[
                vmem((tokens, wide), BF16),
                vmem((tokens, wide), BF16),
                vmem((per, BLK, tokens), BF16),
                vmem((8, LANES), I32),
                vmem((z_n, 8, LANES), I32),
                dma((2,)),
                dma,
                dma((z_n - 1,)),
                dma((z_n - 1,)),
            ],
            compiler_params=params(0),
        )(activations, out_grad, kept_blocks, kept_counts)

        def run(number, room):
            parts = -(-room // PART)
            scratch = [vmem((tokens, narrow), BF16)] * 3 + [
                vmem((3 * fb, tokens, BLK), BF16),
                vmem((BLK, BLK), F32),
                dma((3,)),
                dma((waves,)),
                dma((waves, 2, parts)),
                dma((waves, 2, parts)),
                dma((waves,)),
                dma((waves,)),
                dma((waves,)),
                dma((waves,)),
            ]
            scratch += [vmem((per + 2 * TOP, r, tokens), BF16) for r in ROWS]
            scratch += [vmem((2, room, r, tokens), BF16) for r in ROWS]
            scratch += [vmem((2, room, r, tokens), BF16) for r in ROWS]
            scratch += [vmem((half, r, BLK), F32) for r in ROWS]
            scratch += [vmem((half, r, BLK), F32) for r in ROWS]
            scratch += [vmem((half, r, BLK), F32) for r in ROWS]
            scratch += [vmem((chips, r, BLK), BF16) for r in ROWS]
            scratch += [vmem((chips - 1, r, BLK), BF16) for r in ROWS]
            return pl.pallas_call(
                functools.partial(kernel, (room, dp_n, z_n, tokens, per, fb, slots)),
                out_shape=jax.ShapeDtypeStruct((1, 1, BLK, BLK), F32),
                in_specs=[hbm] * 4 + [smem] * 2,
                out_specs=whole,
                scratch_shapes=scratch,
                compiler_params=params(number),
            )

        longest = plan[4, 0]
        level = sum((longest > room).astype(I32) for room in SIZES[:-1])
        runs = [run(i + 1, room) for i, room in enumerate(SIZES)]
        return lax.switch(level, runs, turned, gate_pre, up_pre, hidden_grad, plan, kept_counts)

    return jax.shard_map(
        per_device,
        mesh=mesh,
        in_specs=(P("dp", "tensor"),) * 5 + (P("tensor", None, None), P("tensor")),
        out_specs=P("dp", "tensor", None, None),
        check_vma=False,
    )
```

```python
import functools

import jax
import jax.numpy as jnp
from jax import lax
from jax.experimental import pallas as pl
from jax.experimental.pallas import tpu as pltpu
from jax.sharding import PartitionSpec as P

BLK = 128
LANES = 128
MESH = pl.DeviceIdType.MESH
ROWS = (32, 32, 32, 16, 16)
BEGIN = (0.0, 0.25, 0.5, 0.8, 1.0)
GROUP = 16
PART = 4
LAG = 2
GAP = PART * LAG
SIZES = (34, 36, 40, 64)
TOP = SIZES[-1]
F32 = jnp.float32
BF16 = jnp.bfloat16
I32 = jnp.int32


def columns(rows):
    rows = list(rows)
    stacked = jnp.concatenate(rows + [rows[0]] * (8 - len(rows)), axis=0)
    turned = jnp.concatenate([stacked] * (LANES // 8), axis=0).T
    return [jnp.broadcast_to(turned[:, i:i + 1], (LANES, LANES)) for i in range(len(rows))]


def plan_kernel(dims, x_hbm, dy_hbm, table, counts, turned, plan, level, x_in, dy_in, t_buf, mine, lists, load_sem, out_sem,
                send_sem, recv_sem):
    z_n, xb, fb, slots = dims
    per = 2 * xb
    dp = lax.axis_index("dp")
    z = lax.axis_index("tensor")

    loads = [pltpu.make_async_copy(src, dst, load_sem.at[i]) for i, (src, dst) in enumerate(((x_hbm, x_in), (dy_hbm, dy_in)))]
    for load in loads:
        load.start()
    barrier = pltpu.get_barrier_semaphore()
    for o in range(1, z_n):
        pl.semaphore_signal(barrier, inc=1, device_id=(dp, lax.rem(z + o, z_n)), device_id_type=MESH)

    m, r, c = (table[i] for i in range(3))
    wide_at = jnp.where(m == 2, c, r)
    narrow_at = jnp.where(m == 2, r, c)
    shift = xb.bit_length() - 1
    ids = jnp.right_shift(wide_at, shift) * per + jnp.where(m == 2, xb, 0) + jnp.bitwise_and(wide_at, xb - 1)
    at = lax.broadcasted_iota(I32, (1, slots), 1)
    mine[...] = jnp.full_like(mine, -1)
    mine[0:1, 0:slots] = jnp.where(at < counts[0], ids, -1)
    lists[z] = mine[...]
    pl.semaphore_wait(barrier, z_n - 1)
    swaps = []
    for o in range(1, z_n):
        swap = pltpu.make_async_remote_copy(
            src_ref=mine, dst_ref=lists.at[z], send_sem=send_sem.at[o - 1], recv_sem=recv_sem.at[o - 1],
            device_id=(dp, lax.rem(z + o, z_n)), device_id_type=MESH)
        swap.start()
        swaps.append(swap)

    def turn(src, base):
        def body(b, _):
            t_buf[base + b] = src[:, pl.ds(pl.multiple_of(b * BLK, BLK), BLK)].T
            return 0

        lax.fori_loop(0, xb, body, 0)

    loads[0].wait()
    turn(x_in, 0)
    loads[1].wait()
    turn(dy_in, xb)
    out = pltpu.make_async_copy(t_buf, turned, out_sem)
    out.start()

    for o, swap in enumerate(swaps):
        pltpu.make_async_remote_copy(
            src_ref=mine, dst_ref=lists.at[lax.rem(z + z_n - o - 1, z_n)], send_sem=send_sem.at[o], recv_sem=recv_sem.at[o],
            device_id=(dp, lax.rem(z + o + 1, z_n)), device_id_type=MESH).wait_recv()

    sub = lax.broadcasted_iota(I32, (LANES, LANES), 0)
    lane = lax.broadcasted_iota(I32, (LANES, LANES), 1)
    pshift = per.bit_length() - 1
    lane_row = lax.broadcasted_iota(I32, (1, LANES), 1)
    src_row = jnp.right_shift(lane_row, pshift)
    blk_row = jnp.bitwise_and(lane_row, per - 1).astype(F32)

    def hits(cond, value=1.0):
        return jnp.sum(jnp.where(cond, value, 0.0), axis=0, keepdims=True)

    need = [jnp.zeros((1, LANES), F32) for _ in range(z_n)]
    lane_f = lane.astype(F32)
    for j, list_col in enumerate(columns(lists[j][0:1].astype(F32) for j in range(z_n))):
        listed = jnp.max(jnp.where(list_col == lane_f, 1.0, 0.0), axis=0, keepdims=True)
        for d in range(z_n):
            need[d] = jnp.where(src_row == (j - d) % z_n, listed, need[d])
    far = z_n // 2
    reach = []
    for way in (0, 1):
        best = jnp.zeros((1, LANES), F32)
        for d in range(1, far):
            best = jnp.maximum(best, d * need[d if way == 0 else z_n - d])
        reach.append(best)
    odd = jnp.bitwise_and(lane_row, 1).astype(F32)
    lead = reach[0] - reach[1] + 0.5 - odd
    reach = [
        jnp.where(lead > 0, jnp.maximum(reach[0], far * need[far]), reach[0]),
        jnp.where(lead > 0, reach[1], jnp.maximum(reach[1], far * need[far])),
    ]

    same = jnp.right_shift(sub, pshift) == jnp.right_shift(lane, pshift)
    longest = jnp.zeros((1, 1), F32)
    places, puts = [], []
    for way, reach_col in enumerate(columns(reach)):
        ahead = jnp.logical_or(reach_col > reach[way], jnp.logical_and(reach_col == reach[way], sub < lane))
        rank = hits(jnp.logical_and(same, ahead))
        number = [None] + [hits(jnp.logical_and(same, reach_col >= d)) for d in range(1, far + 1)]

        def from_back(row, places_back):
            step = per * places_back if way == 0 else LANES - per * places_back
            full = pltpu.roll(jnp.broadcast_to(row, (8, LANES)), step % LANES, 1)
            return full[0:1]

        start = [None, jnp.zeros((1, LANES), F32)]
        for d in range(2, far + 1):
            before = number[d - 1] if d == 2 else from_back(number[d - 1], d - 2)
            lag = start[d - 1] if d == 2 else from_back(start[d - 1], 1)
            start.append(jnp.maximum(start[d - 1] + before, lag + GAP))
        length = start[far] + from_back(number[far], far - 1)
        longest = jnp.maximum(longest, jnp.max(length, axis=1, keepdims=True))

        def of(row, shard):
            return jnp.max(jnp.where(src_row == shard, row, 0.0), axis=1, keepdims=True)

        back = lax.rem(z + (z_n - 1 if way == 0 else 1), z_n)
        away = jnp.bitwise_and(z - src_row + z_n, z_n - 1)
        if way == 1:
            away = jnp.bitwise_and(z_n - away, z_n - 1)
        got, put = rank, rank
        for d in range(2, far + 1):
            got = got + jnp.where(away == d, of(start[d], back), 0.0)
            put = put + jnp.where(away == d - 1, of(start[d], z), 0.0)
        place = jnp.where(away == 0, blk_row, per + TOP * way + got)
        away_f = away.astype(F32)
        put = jnp.where(jnp.logical_and(away_f < far, reach[way] > away_f), put, -1.0)
        puts.append(put)
        places.append(place)

    away = jnp.bitwise_and(z - src_row + z_n, z_n - 1)
    opposite = jnp.where(reach[0] == float(far), places[0], places[1])
    place = jnp.where(away < far, places[0], jnp.where(away == far, opposite, places[1]))
    put_cols = columns(puts + places + [place])
    orders = [hits(put_cols[way] == lane_f, put_cols[2 + way]) for way in (0, 1)]
    at_slot = hits(sub == mine[0:1], put_cols[4])

    plan[...] = jnp.zeros_like(plan)
    plan[0:1, :] = orders[0].astype(I32)
    plan[1:2, :] = orders[1].astype(I32)
    plan[2:3, :] = at_slot.astype(I32)
    plan[3:4, 0:slots] = m * fb + narrow_at
    top = jnp.max(longest)
    level[0] = sum(jnp.where(top > room, 1, 0) for room in SIZES[:-1])
    for swap in swaps:
        swap.wait_send()
    out.wait()


def kernel(dims, turned, gate_hbm, up_hbm, grad_hbm, plan, counts, out_ref, gate_in, up_in, grad_in,
           f_buf, acc, load_sem, own_sem, ring_send, ring_recv, pair_send, pair_recv, sum_send, sum_recv, *bufs):
    room, dp_n, z_n, tokens, per, fb, slots = dims
    waves = len(ROWS)
    held = bufs[0:waves]
    stage = bufs[waves:2 * waves]
    came = bufs[2 * waves:3 * waves]
    p_out = bufs[3 * waves:4 * waves]
    p_own = bufs[4 * waves:5 * waves]
    p_in = bufs[5 * waves:6 * waves]
    s_buf = bufs[6 * waves:7 * waves]
    r_buf = bufs[7 * waves:8 * waves]
    chips = dp_n // 2
    half = slots // 2

    dp = lax.axis_index("dp")
    z = lax.axis_index("tensor")
    core = lax.rem(dp, 2)
    chip = lax.div(dp, 2)
    sibling = dp + 1 - 2 * core
    right, left = lax.rem(z + 1, z_n), lax.rem(z + z_n - 1, z_n)
    starts = [sum(ROWS[:w]) for w in range(waves)]

    own = [
        pltpu.make_async_copy(turned.at[:, pl.ds(starts[w], ROWS[w])], held[w].at[pl.ds(0, per)], own_sem.at[w])
        for w in range(waves)
    ]
    for load in own:
        load.start()
    loads = [
        pltpu.make_async_copy(src, dst, load_sem.at[i])
        for i, (src, dst) in enumerate(((gate_hbm, gate_in), (up_hbm, up_in), (grad_hbm, grad_in)))
    ]
    for load in loads:
        load.start()

    barrier = pltpu.get_barrier_semaphore()
    for to in (left, right):
        pl.semaphore_signal(barrier, inc=1, device_id=(dp, to), device_id_type=MESH)
    pl.semaphore_signal(barrier, inc=1, device_id=(sibling, z), device_id_type=MESH)

    def greet(o, _):
        pl.semaphore_signal(barrier, inc=1, device_id=(lax.rem(chip + o, chips) * 2 + core, z), device_id_type=MESH)
        return 0

    lax.fori_loop(1, chips, greet, 0)

    cuts = [(p, min(p + PART, room)) for p in range(0, room, PART)]
    parts = len(cuts)

    def message(w, way, q):
        first, last = cuts[q]
        cut = pl.ds(first, last - first)
        return pltpu.make_async_remote_copy(
            src_ref=stage[w].at[way, cut], dst_ref=came[w].at[way, cut],
            send_sem=ring_send.at[w, way, q], recv_sem=ring_recv.at[w, way, q],
            device_id=(dp, right if way == 0 else left), device_id_type=MESH)

    def fill(w, q):
        for p in range(*cuts[q]):
            for way in (0, 1):
                stage[w][way, p] = held[w][plan[way, p]]

    def send(w, q):
        fill(w, q)
        for way in (0, 1):
            message(w, way, q).start()

    def take(w, q):
        for way in (0, 1):
            message(w, way, q).wait_recv()

        first, last = cuts[q]
        for way in (0, 1):
            at = per + TOP * way
            held[w][at + first:at + last] = came[w][way, first:last]

    def back(f, _):
        cols = pl.ds(pl.multiple_of(f * BLK, BLK), BLK)
        g = gate_in[:, cols].astype(F32)
        u = up_in[:, cols].astype(F32)
        d = grad_in[:, cols].astype(F32)
        s = 1.0 / (1.0 + jnp.exp(-g))
        active = g * s
        f_buf[f] = (d * u * s * (1.0 + g * (1.0 - s))).astype(BF16)
        f_buf[fb + f] = (d * active).astype(BF16)
        f_buf[2 * fb + f] = (active * u).astype(BF16)
        return 0

    def products(w, dst, parity):
        def body(i, _):
            for j in range(GROUP):
                n = i * GROUP + j
                k = 2 * n + parity
                dst[n] = jnp.dot(held[w][plan[2, k]], f_buf[plan[3, k]], preferred_element_type=F32)
            return 0

        lax.fori_loop(0, half // GROUP, body, 0)

    def pair(w):
        return pltpu.make_async_remote_copy(
            src_ref=p_out[w], dst_ref=p_in[w], send_sem=pair_send.at[w], recv_sem=pair_recv.at[w],
            device_id=(sibling, z), device_id_type=MESH)

    def spread(w):
        pair(w).wait_recv()

        def add(n, _):
            s_buf[w][n] = (p_own[w][n] + p_in[w][n]).astype(BF16)
            return 0

        lax.fori_loop(0, chips, add, 0)

        def post(o, _):
            to = lax.rem(chip + o, chips)
            pltpu.make_async_remote_copy(
                src_ref=s_buf[w].at[to], dst_ref=r_buf[w].at[o - 1], send_sem=sum_send.at[w], recv_sem=sum_recv.at[w],
                device_id=(to * 2 + core, z), device_id_type=MESH).start()
            return 0

        lax.fori_loop(1, chips, post, 0)

    def all_sums(w):
        return pltpu.make_async_remote_copy(
            src_ref=s_buf[w].at[pl.ds(0, chips - 1)], dst_ref=r_buf[w], send_sem=sum_send.at[w], recv_sem=sum_recv.at[w],
            device_id=(sibling, z), device_id_type=MESH)

    def collect(w):
        all_sums(w).wait_recv()
        total = p_own[w][chip] + p_in[w][chip]
        for o in range(chips - 1):
            total = total + r_buf[w][o].astype(F32)
        acc[pl.ds(starts[w], ROWS[w])] = total

    def make_sib(w):
        products(w, p_out[w], 1 - core)
        pair(w).start()

    def make_own(w):
        products(w, p_own[w], core)

    events = sorted((BEGIN[w] * parts + q, w, q) for w in range(waves) for q in range(parts + LAG))
    todo = []
    for i, (_, w, q) in enumerate(events):
        if q >= LAG:
            take(w, q - LAG)
        if q == 0:
            own[w].wait()
        if q < parts:
            if i == 0:
                fill(w, q)
                pl.semaphore_wait(barrier, 3 + chips - 1)
                for way in (0, 1):
                    message(w, way, q).start()
            else:
                send(w, q)
        if i == LAG - 1:
            for load in loads:
                load.wait()
            lax.fori_loop(0, fb, back, 0)
        if q == parts + LAG - 1:
            todo += [(i, make_sib, w), (i + 1, make_own, w), (i + 5, spread, w)]
        while todo and todo[0][0] <= i:
            _, task, which = todo.pop(0)
            task(which)
        todo.sort(key=lambda entry: entry[0])
    for _, task, which in todo:
        task(which)
    for w in range(waves):
        collect(w)

    value = acc[...]
    down = plan[3, dp] >= 2 * fb
    value = jnp.where(down, value.T, value)
    scale = float(tokens * dp_n) ** (-0.5)
    live = (dp < counts[0]).astype(F32)
    out_ref[0, 0] = value * scale * live

    for w in range(waves):
        for q in range(parts):
            for way in (0, 1):
                message(w, way, q).wait_send()
    for w in range(waves):
        pair(w).wait_send()
        all_sums(w).wait_send()


def solution(mesh):
    dp_n, z_n = mesh.shape["dp"], mesh.shape["tensor"]
    vmem = pltpu.VMEM
    dma = pltpu.SemaphoreType.DMA
    hbm = pl.BlockSpec(memory_space=pl.ANY)
    smem = pl.BlockSpec(memory_space=pltpu.SMEM)
    whole = pl.BlockSpec(memory_space=pltpu.VMEM)

    def params(number):
        return pltpu.CompilerParams(collective_id=number, has_side_effects=True, vmem_limit_bytes=62 * 1024 * 1024)

    def per_device(activations, out_grad, gate_pre, up_pre, hidden_grad, kept_blocks, kept_counts):
        tokens, wide = activations.shape
        narrow = gate_pre.shape[1]
        slots = kept_blocks.shape[2]
        chips, half = dp_n // 2, slots // 2
        xb, fb = wide // BLK, narrow // BLK
        per = 2 * xb
        waves = len(ROWS)
        turned, plan, level = pl.pallas_call(
            functools.partial(plan_kernel, (z_n, xb, fb, slots)),
            out_shape=(
                jax.ShapeDtypeStruct((per, BLK, tokens), BF16),
                jax.ShapeDtypeStruct((8, LANES), I32),
                jax.ShapeDtypeStruct((1,), I32),
            ),
            in_specs=[hbm, hbm, whole, smem],
            out_specs=(hbm, whole, smem),
            scratch_shapes=[
                vmem((tokens, wide), BF16),
                vmem((tokens, wide), BF16),
                vmem((per, BLK, tokens), BF16),
                vmem((8, LANES), I32),
                vmem((z_n, 8, LANES), I32),
                dma((2,)),
                dma,
                dma((z_n - 1,)),
                dma((z_n - 1,)),
            ],
            compiler_params=params(0),
        )(activations, out_grad, kept_blocks.transpose(1, 0, 2), kept_counts)

        def run(number, room):
            parts = -(-room // PART)
            scratch = [vmem((tokens, narrow), BF16)] * 3 + [
                vmem((3 * fb, tokens, BLK), BF16),
                vmem((BLK, BLK), F32),
                dma((3,)),
                dma((waves,)),
                dma((waves, 2, parts)),
                dma((waves, 2, parts)),
                dma((waves,)),
                dma((waves,)),
                dma((waves,)),
                dma((waves,)),
            ]
            scratch += [vmem((per + 2 * TOP, r, tokens), BF16) for r in ROWS]
            scratch += [vmem((2, room, r, tokens), BF16) for r in ROWS]
            scratch += [vmem((2, room, r, tokens), BF16) for r in ROWS]
            scratch += [vmem((half, r, BLK), F32) for r in ROWS]
            scratch += [vmem((half, r, BLK), F32) for r in ROWS]
            scratch += [vmem((half, r, BLK), F32) for r in ROWS]
            scratch += [vmem((chips, r, BLK), BF16) for r in ROWS]
            scratch += [vmem((chips - 1, r, BLK), BF16) for r in ROWS]
            return pl.pallas_call(
                functools.partial(kernel, (room, dp_n, z_n, tokens, per, fb, slots)),
                out_shape=jax.ShapeDtypeStruct((1, 1, BLK, BLK), F32),
                in_specs=[hbm] * 4 + [smem] * 2,
                out_specs=whole,
                scratch_shapes=scratch,
                compiler_params=params(number),
            )

        runs = [run(i + 1, room) for i, room in enumerate(SIZES)]
        return lax.switch(level[0], runs, turned, gate_pre, up_pre, hidden_grad, plan, kept_counts)

    return jax.shard_map(
        per_device,
        mesh=mesh,
        in_specs=(P("dp", "tensor"),) * 5 + (P("tensor", None, None), P("tensor")),
        out_specs=P("dp", "tensor", None, None),
        check_vma=False,
    )
```

```python
import functools

import jax
import jax.numpy as jnp
from jax import lax
from jax.experimental import pallas as pl
from jax.experimental.pallas import tpu as pltpu
from jax.sharding import PartitionSpec as P

BLK = 128
LANES = 128
MESH = pl.DeviceIdType.MESH
ROWS = (32, 32, 32, 16, 16)
BEGIN = (0.0, 0.25, 0.5, 0.8, 1.0)
GROUP = 16
PART = 4
LAG = 2
GAP = PART * LAG
SIZES = (32, 34, 36, 39, 64)
TOP = SIZES[-1]
F32 = jnp.float32
BF16 = jnp.bfloat16
I32 = jnp.int32


def columns(rows):
    rows = list(rows)
    stacked = jnp.concatenate(rows + [rows[0]] * (8 - len(rows)), axis=0)
    turned = jnp.concatenate([stacked] * (LANES // 8), axis=0).T
    return [jnp.broadcast_to(turned[:, i:i + 1], (LANES, LANES)) for i in range(len(rows))]


def plan_kernel(dims, x_hbm, dy_hbm, table, counts, turned, plan, level, x_in, dy_in, t_buf, mine, lists, load_sem, out_sem,
                send_sem, recv_sem):
    z_n, xb, fb, slots = dims
    per = 2 * xb
    dp = lax.axis_index("dp")
    z = lax.axis_index("tensor")

    loads = [pltpu.make_async_copy(src, dst, load_sem.at[i]) for i, (src, dst) in enumerate(((x_hbm, x_in), (dy_hbm, dy_in)))]
    for load in loads:
        load.start()
    barrier = pltpu.get_barrier_semaphore()
    for o in range(1, z_n):
        pl.semaphore_signal(barrier, inc=1, device_id=(dp, lax.rem(z + o, z_n)), device_id_type=MESH)

    m, r, c = (table[i] for i in range(3))
    wide_at = jnp.where(m == 2, c, r)
    narrow_at = jnp.where(m == 2, r, c)
    shift = xb.bit_length() - 1
    ids = jnp.right_shift(wide_at, shift) * per + jnp.where(m == 2, xb, 0) + jnp.bitwise_and(wide_at, xb - 1)
    at = lax.broadcasted_iota(I32, (1, slots), 1)
    mine[...] = jnp.full_like(mine, -1)
    mine[0:1, 0:slots] = jnp.where(at < counts[0], ids, -1)
    lists[z] = mine[...]
    pl.semaphore_wait(barrier, z_n - 1)
    swaps = []
    for o in range(1, z_n):
        swap = pltpu.make_async_remote_copy(
            src_ref=mine, dst_ref=lists.at[z], send_sem=send_sem.at[o - 1], recv_sem=recv_sem.at[o - 1],
            device_id=(dp, lax.rem(z + o, z_n)), device_id_type=MESH)
        swap.start()
        swaps.append(swap)

    def turn(src, base):
        def body(b, _):
            t_buf[base + b] = src[:, pl.ds(pl.multiple_of(b * BLK, BLK), BLK)].T
            return 0

        lax.fori_loop(0, xb, body, 0)

    loads[0].wait()
    turn(x_in, 0)
    loads[1].wait()
    turn(dy_in, xb)
    out = pltpu.make_async_copy(t_buf, turned, out_sem)
    out.start()

    for o, swap in enumerate(swaps):
        pltpu.make_async_remote_copy(
            src_ref=mine, dst_ref=lists.at[lax.rem(z + z_n - o - 1, z_n)], send_sem=send_sem.at[o], recv_sem=recv_sem.at[o],
            device_id=(dp, lax.rem(z + o + 1, z_n)), device_id_type=MESH).wait_recv()

    sub = lax.broadcasted_iota(I32, (LANES, LANES), 0)
    lane = lax.broadcasted_iota(I32, (LANES, LANES), 1)
    pshift = per.bit_length() - 1
    lane_row = lax.broadcasted_iota(I32, (1, LANES), 1)
    src_row = jnp.right_shift(lane_row, pshift)
    blk_row = jnp.bitwise_and(lane_row, per - 1).astype(F32)

    def hits(cond, value=1.0):
        return jnp.sum(jnp.where(cond, value, 0.0), axis=0, keepdims=True)

    need = [jnp.zeros((1, LANES), F32) for _ in range(z_n)]
    lane_f = lane.astype(F32)
    for j, list_col in enumerate(columns(lists[j][0:1].astype(F32) for j in range(z_n))):
        listed = jnp.max(jnp.where(list_col == lane_f, 1.0, 0.0), axis=0, keepdims=True)
        for d in range(z_n):
            need[d] = jnp.where(src_row == (j - d) % z_n, listed, need[d])
    far = z_n // 2
    reach = []
    for way in (0, 1):
        best = jnp.zeros((1, LANES), F32)
        for d in range(1, far):
            best = jnp.maximum(best, d * need[d if way == 0 else z_n - d])
        reach.append(best)
    same = jnp.right_shift(sub, pshift) == jnp.right_shift(lane, pshift)
    same_f = jnp.where(same, 1.0, 0.0)

    def numbers(depth):
        rows = [jnp.where(reach[way] >= d, 1.0, 0.0) for way in (0, 1) for d in range(1, depth + 1)]
        stacked = jnp.concatenate(rows + [rows[0]] * (8 - len(rows)), axis=0)
        total = jnp.dot(stacked, same_f, preferred_element_type=F32)
        return [[None] + [total[way * depth + d:way * depth + d + 1] for d in range(depth)] for way in (0, 1)]

    def from_back(way, row, back):
        step = per * (back % z_n)
        step = step if way == 0 else (LANES - step) % LANES
        return row if step == 0 else pltpu.roll(jnp.broadcast_to(row, (8, LANES)), step, 1)[0:1]

    beyond = []
    for way, number in enumerate(numbers(far - 1)):
        load = sum(from_back(way, number[d], d - 1) for d in range(1, far))
        beyond.append(sum(jnp.where(reach[way] <= e, from_back(way, load, -e), 0.0) for e in range(far)))
    odd = jnp.bitwise_and(lane_row, 1).astype(F32)
    lead = beyond[1] - beyond[0] + 0.5 - odd
    reach = [
        jnp.where(lead > 0, jnp.maximum(reach[0], far * need[far]), reach[0]),
        jnp.where(lead > 0, reach[1], jnp.maximum(reach[1], far * need[far])),
    ]

    longest = jnp.zeros((1, 1), F32)
    places, puts = [], []
    for way, (reach_col, number) in enumerate(zip(columns(reach), numbers(far))):
        ahead = jnp.logical_or(reach_col > reach[way], jnp.logical_and(reach_col == reach[way], sub < lane))
        rank = hits(jnp.logical_and(same, ahead))

        start = [None, jnp.zeros((1, LANES), F32)]
        for d in range(2, far + 1):
            before = from_back(way, number[d - 1], d - 2)
            start.append(jnp.maximum(start[d - 1] + before, from_back(way, start[d - 1], 1) + GAP))
        length = start[far] + from_back(way, number[far], far - 1)
        longest = jnp.maximum(longest, jnp.max(length, axis=1, keepdims=True))

        def of(row, shard):
            return jnp.max(jnp.where(src_row == shard, row, 0.0), axis=1, keepdims=True)

        back = lax.rem(z + (z_n - 1 if way == 0 else 1), z_n)
        away = jnp.bitwise_and(z - src_row + z_n, z_n - 1)
        if way == 1:
            away = jnp.bitwise_and(z_n - away, z_n - 1)
        got, put = rank, rank
        for d in range(2, far + 1):
            got = got + jnp.where(away == d, of(start[d], back), 0.0)
            put = put + jnp.where(away == d - 1, of(start[d], z), 0.0)
        place = jnp.where(away == 0, blk_row, per + TOP * way + got)
        away_f = away.astype(F32)
        put = jnp.where(jnp.logical_and(away_f < far, reach[way] > away_f), put, -1.0)
        puts.append(put)
        places.append(place)

    away = jnp.bitwise_and(z - src_row + z_n, z_n - 1)
    opposite = jnp.where(reach[0] == float(far), places[0], places[1])
    place = jnp.where(away < far, places[0], jnp.where(away == far, opposite, places[1]))
    put_cols = columns(puts + places + [place])
    orders = [hits(put_cols[way] == lane_f, put_cols[2 + way]) for way in (0, 1)]
    at_slot = hits(sub == mine[0:1], put_cols[4])

    plan[...] = jnp.zeros_like(plan)
    plan[0:1, :] = orders[0].astype(I32)
    plan[1:2, :] = orders[1].astype(I32)
    plan[2:3, :] = at_slot.astype(I32)
    plan[3:4, 0:slots] = m * fb + narrow_at
    top = jnp.max(longest)
    level[0] = sum(jnp.where(top > room, 1, 0) for room in SIZES[:-1])
    for swap in swaps:
        swap.wait_send()
    out.wait()


def kernel(dims, turned, gate_hbm, up_hbm, grad_hbm, plan, counts, out_ref, gate_in, up_in, grad_in,
           f_buf, acc, load_sem, own_sem, ring_send, ring_recv, pair_send, pair_recv, sum_send, sum_recv, *bufs):
    room, dp_n, z_n, tokens, per, fb, slots = dims
    waves = len(ROWS)
    held = bufs[0:waves]
    stage = bufs[waves:2 * waves]
    came = bufs[2 * waves:3 * waves]
    p_out = bufs[3 * waves:4 * waves]
    p_own = bufs[4 * waves:5 * waves]
    p_in = bufs[5 * waves:6 * waves]
    s_buf = bufs[6 * waves:7 * waves]
    r_buf = bufs[7 * waves:8 * waves]
    chips = dp_n // 2
    half = slots // 2

    dp = lax.axis_index("dp")
    z = lax.axis_index("tensor")
    core = lax.rem(dp, 2)
    chip = lax.div(dp, 2)
    sibling = dp + 1 - 2 * core
    right, left = lax.rem(z + 1, z_n), lax.rem(z + z_n - 1, z_n)
    starts = [sum(ROWS[:w]) for w in range(waves)]

    own = [
        pltpu.make_async_copy(turned.at[:, pl.ds(starts[w], ROWS[w])], held[w].at[pl.ds(0, per)], own_sem.at[w])
        for w in range(waves)
    ]
    for load in own:
        load.start()
    loads = [
        pltpu.make_async_copy(src, dst, load_sem.at[i])
        for i, (src, dst) in enumerate(((gate_hbm, gate_in), (up_hbm, up_in), (grad_hbm, grad_in)))
    ]
    for load in loads:
        load.start()

    barrier = pltpu.get_barrier_semaphore()
    for to in (left, right):
        pl.semaphore_signal(barrier, inc=1, device_id=(dp, to), device_id_type=MESH)
    pl.semaphore_signal(barrier, inc=1, device_id=(sibling, z), device_id_type=MESH)

    def greet(o, _):
        pl.semaphore_signal(barrier, inc=1, device_id=(lax.rem(chip + o, chips) * 2 + core, z), device_id_type=MESH)
        return 0

    lax.fori_loop(1, chips, greet, 0)

    cuts = [(p, min(p + PART, room)) for p in range(0, room, PART)]
    parts = len(cuts)

    def message(w, way, q):
        first, last = cuts[q]
        cut = pl.ds(first, last - first)
        return pltpu.make_async_remote_copy(
            src_ref=stage[w].at[way, cut], dst_ref=came[w].at[way, cut],
            send_sem=ring_send.at[w, way, q], recv_sem=ring_recv.at[w, way, q],
            device_id=(dp, right if way == 0 else left), device_id_type=MESH)

    def fill(w, q):
        for p in range(*cuts[q]):
            for way in (0, 1):
                stage[w][way, p] = held[w][plan[way, p]]

    def send(w, q):
        fill(w, q)
        for way in (0, 1):
            message(w, way, q).start()

    def take(w, q):
        for way in (0, 1):
            message(w, way, q).wait_recv()

        first, last = cuts[q]
        for way in (0, 1):
            at = per + TOP * way
            held[w][at + first:at + last] = came[w][way, first:last]

    def back(f, _):
        cols = pl.ds(pl.multiple_of(f * BLK, BLK), BLK)
        g = gate_in[:, cols].astype(F32)
        u = up_in[:, cols].astype(F32)
        d = grad_in[:, cols].astype(F32)
        s = 1.0 / (1.0 + jnp.exp(-g))
        active = g * s
        f_buf[f] = (d * u * s * (1.0 + g * (1.0 - s))).astype(BF16)
        f_buf[fb + f] = (d * active).astype(BF16)
        f_buf[2 * fb + f] = (active * u).astype(BF16)
        return 0

    def products(w, dst, parity):
        def body(i, _):
            for j in range(GROUP):
                n = i * GROUP + j
                k = 2 * n + parity
                dst[n] = jnp.dot(held[w][plan[2, k]], f_buf[plan[3, k]], preferred_element_type=F32)
            return 0

        lax.fori_loop(0, half // GROUP, body, 0)

    def pair(w):
        return pltpu.make_async_remote_copy(
            src_ref=p_out[w], dst_ref=p_in[w], send_sem=pair_send.at[w], recv_sem=pair_recv.at[w],
            device_id=(sibling, z), device_id_type=MESH)

    def spread(w):
        pair(w).wait_recv()

        def add(n, _):
            s_buf[w][n] = (p_own[w][n] + p_in[w][n]).astype(BF16)
            return 0

        lax.fori_loop(0, chips, add, 0)

        def post(o, _):
            to = lax.rem(chip + o, chips)
            pltpu.make_async_remote_copy(
                src_ref=s_buf[w].at[to], dst_ref=r_buf[w].at[o - 1], send_sem=sum_send.at[w], recv_sem=sum_recv.at[w],
                device_id=(to * 2 + core, z), device_id_type=MESH).start()
            return 0

        lax.fori_loop(1, chips, post, 0)

    def all_sums(w):
        return pltpu.make_async_remote_copy(
            src_ref=s_buf[w].at[pl.ds(0, chips - 1)], dst_ref=r_buf[w], send_sem=sum_send.at[w], recv_sem=sum_recv.at[w],
            device_id=(sibling, z), device_id_type=MESH)

    def collect(w):
        all_sums(w).wait_recv()
        total = p_own[w][chip] + p_in[w][chip]
        for o in range(chips - 1):
            total = total + r_buf[w][o].astype(F32)
        acc[pl.ds(starts[w], ROWS[w])] = total

    def make_sib(w):
        products(w, p_out[w], 1 - core)
        pair(w).start()

    def make_own(w):
        products(w, p_own[w], core)

    events = sorted((BEGIN[w] * parts + q, w, q) for w in range(waves) for q in range(parts + LAG))
    todo = []
    for i, (_, w, q) in enumerate(events):
        if q >= LAG:
            take(w, q - LAG)
        if q == 0:
            own[w].wait()
        if q < parts:
            if i == 0:
                fill(w, q)
                pl.semaphore_wait(barrier, 3 + chips - 1)
                for way in (0, 1):
                    message(w, way, q).start()
            else:
                send(w, q)
        if i == LAG - 1:
            for load in loads:
                load.wait()
            lax.fori_loop(0, fb, back, 0)
        if q == parts + LAG - 1:
            todo += [(i, make_sib, w), (i + 1, make_own, w), (i + 5, spread, w)]
        while todo and todo[0][0] <= i:
            _, task, which = todo.pop(0)
            task(which)
        todo.sort(key=lambda entry: entry[0])
    for _, task, which in todo:
        task(which)
    for w in range(waves):
        collect(w)

    value = acc[...]
    down = plan[3, dp] >= 2 * fb
    value = jnp.where(down, value.T, value)
    scale = float(tokens * dp_n) ** (-0.5)
    live = (dp < counts[0]).astype(F32)
    out_ref[0, 0] = value * scale * live

    for w in range(waves):
        for q in range(parts):
            for way in (0, 1):
                message(w, way, q).wait_send()
    for w in range(waves):
        pair(w).wait_send()
        all_sums(w).wait_send()


def solution(mesh):
    dp_n, z_n = mesh.shape["dp"], mesh.shape["tensor"]
    vmem = pltpu.VMEM
    dma = pltpu.SemaphoreType.DMA
    hbm = pl.BlockSpec(memory_space=pl.ANY)
    smem = pl.BlockSpec(memory_space=pltpu.SMEM)
    whole = pl.BlockSpec(memory_space=pltpu.VMEM)

    def params(number):
        return pltpu.CompilerParams(collective_id=number, has_side_effects=True, vmem_limit_bytes=62 * 1024 * 1024)

    def per_device(activations, out_grad, gate_pre, up_pre, hidden_grad, kept_blocks, kept_counts):
        tokens, wide = activations.shape
        narrow = gate_pre.shape[1]
        slots = kept_blocks.shape[2]
        chips, half = dp_n // 2, slots // 2
        xb, fb = wide // BLK, narrow // BLK
        per = 2 * xb
        waves = len(ROWS)
        turned, plan, level = pl.pallas_call(
            functools.partial(plan_kernel, (z_n, xb, fb, slots)),
            out_shape=(
                jax.ShapeDtypeStruct((per, BLK, tokens), BF16),
                jax.ShapeDtypeStruct((8, LANES), I32),
                jax.ShapeDtypeStruct((1,), I32),
            ),
            in_specs=[hbm, hbm, whole, smem],
            out_specs=(hbm, whole, smem),
            scratch_shapes=[
                vmem((tokens, wide), BF16),
                vmem((tokens, wide), BF16),
                vmem((per, BLK, tokens), BF16),
                vmem((8, LANES), I32),
                vmem((z_n, 8, LANES), I32),
                dma((2,)),
                dma,
                dma((z_n - 1,)),
                dma((z_n - 1,)),
            ],
            compiler_params=params(0),
        )(activations, out_grad, kept_blocks.transpose(1, 0, 2), kept_counts)

        def run(number, room):
            parts = -(-room // PART)
            scratch = [vmem((tokens, narrow), BF16)] * 3 + [
                vmem((3 * fb, tokens, BLK), BF16),
                vmem((BLK, BLK), F32),
                dma((3,)),
                dma((waves,)),
                dma((waves, 2, parts)),
                dma((waves, 2, parts)),
                dma((waves,)),
                dma((waves,)),
                dma((waves,)),
                dma((waves,)),
            ]
            scratch += [vmem((per + 2 * TOP, r, tokens), BF16) for r in ROWS]
            scratch += [vmem((2, room, r, tokens), BF16) for r in ROWS]
            scratch += [vmem((2, room, r, tokens), BF16) for r in ROWS]
            scratch += [vmem((half, r, BLK), F32) for r in ROWS]
            scratch += [vmem((half, r, BLK), F32) for r in ROWS]
            scratch += [vmem((half, r, BLK), F32) for r in ROWS]
            scratch += [vmem((chips, r, BLK), BF16) for r in ROWS]
            scratch += [vmem((chips - 1, r, BLK), BF16) for r in ROWS]
            return pl.pallas_call(
                functools.partial(kernel, (room, dp_n, z_n, tokens, per, fb, slots)),
                out_shape=jax.ShapeDtypeStruct((1, 1, BLK, BLK), F32),
                in_specs=[hbm] * 4 + [smem] * 2,
                out_specs=whole,
                scratch_shapes=scratch,
                compiler_params=params(number),
            )

        runs = [run(i + 1, room) for i, room in enumerate(SIZES)]
        return lax.switch(level[0], runs, turned, gate_pre, up_pre, hidden_grad, plan, kept_counts)

    return jax.shard_map(
        per_device,
        mesh=mesh,
        in_specs=(P("dp", "tensor"),) * 5 + (P("tensor", None, None), P("tensor")),
        out_specs=P("dp", "tensor", None, None),
        check_vma=False,
    )
```

```python
import functools

import jax
import jax.numpy as jnp
from jax import lax
from jax.experimental import pallas as pl
from jax.experimental.pallas import tpu as pltpu
from jax.sharding import PartitionSpec as P

BLK = 128
LANES = 128
MESH = pl.DeviceIdType.MESH
ROWS = (32, 32, 32, 16, 16)
BEGIN = (0.0, 0.25, 0.5, 0.8, 1.0)
GROUP = 16
PART = 4
LAG = 2
GAP = PART * LAG
SIZES = (32, 34, 36, 39, 64)
TOP = SIZES[-1]
F32 = jnp.float32
BF16 = jnp.bfloat16
I32 = jnp.int32


def columns(rows):
    rows = list(rows)
    stacked = jnp.concatenate(rows + [rows[0]] * (8 - len(rows)), axis=0)
    turned = jnp.concatenate([stacked] * (LANES // 8), axis=0).T
    return [jnp.broadcast_to(turned[:, i:i + 1], (LANES, LANES)) for i in range(len(rows))]


def plan_kernel(dims, x_hbm, dy_hbm, table, counts, turned, plan, level, x_in, dy_in, t_buf, mine, lists, load_sem, out_sem,
                send_sem, recv_sem):
    z_n, xb, fb, slots = dims
    per = 2 * xb
    dp = lax.axis_index("dp")
    z = lax.axis_index("tensor")

    loads = [pltpu.make_async_copy(src, dst, load_sem.at[i]) for i, (src, dst) in enumerate(((x_hbm, x_in), (dy_hbm, dy_in)))]
    for load in loads:
        load.start()
    barrier = pltpu.get_barrier_semaphore()
    for o in range(1, z_n):
        pl.semaphore_signal(barrier, inc=1, device_id=(dp, lax.rem(z + o, z_n)), device_id_type=MESH)

    m, r, c = (table[i] for i in range(3))
    wide_at = jnp.where(m == 2, c, r)
    narrow_at = jnp.where(m == 2, r, c)
    shift = xb.bit_length() - 1
    ids = jnp.right_shift(wide_at, shift) * per + jnp.where(m == 2, xb, 0) + jnp.bitwise_and(wide_at, xb - 1)
    at = lax.broadcasted_iota(I32, (1, slots), 1)
    mine[...] = jnp.full_like(mine, -1)
    mine[0:1, 0:slots] = jnp.where(at < counts[0], ids, -1)
    lists[z] = mine[...]
    pl.semaphore_wait(barrier, z_n - 1)
    swaps = []
    for o in range(1, z_n):
        swap = pltpu.make_async_remote_copy(
            src_ref=mine, dst_ref=lists.at[z], send_sem=send_sem.at[o - 1], recv_sem=recv_sem.at[o - 1],
            device_id=(dp, lax.rem(z + o, z_n)), device_id_type=MESH)
        swap.start()
        swaps.append(swap)

    def turn(src, base):
        def body(b, _):
            t_buf[base + b] = src[:, pl.ds(pl.multiple_of(b * BLK, BLK), BLK)].T
            return 0

        lax.fori_loop(0, xb, body, 0)

    loads[0].wait()
    turn(x_in, 0)
    loads[1].wait()
    turn(dy_in, xb)
    out = pltpu.make_async_copy(t_buf, turned, out_sem)
    out.start()

    for o, swap in enumerate(swaps):
        pltpu.make_async_remote_copy(
            src_ref=mine, dst_ref=lists.at[lax.rem(z + z_n - o - 1, z_n)], send_sem=send_sem.at[o], recv_sem=recv_sem.at[o],
            device_id=(dp, lax.rem(z + o + 1, z_n)), device_id_type=MESH).wait_recv()

    sub = lax.broadcasted_iota(I32, (LANES, LANES), 0)
    lane = lax.broadcasted_iota(I32, (LANES, LANES), 1)
    pshift = per.bit_length() - 1
    lane_row = lax.broadcasted_iota(I32, (1, LANES), 1)
    src_row = jnp.right_shift(lane_row, pshift)
    blk_row = jnp.bitwise_and(lane_row, per - 1).astype(F32)

    def hits(cond, value=1.0):
        return jnp.sum(jnp.where(cond, value, 0.0), axis=0, keepdims=True)

    need = [jnp.zeros((1, LANES), F32) for _ in range(z_n)]
    lane_f = lane.astype(F32)
    for j, list_col in enumerate(columns(lists[j][0:1].astype(F32) for j in range(z_n))):
        listed = jnp.max(jnp.where(list_col == lane_f, 1.0, 0.0), axis=0, keepdims=True)
        for d in range(z_n):
            need[d] = jnp.where(src_row == (j - d) % z_n, listed, need[d])
    far = z_n // 2
    reach = []
    for way in (0, 1):
        best = jnp.zeros((1, LANES), F32)
        for d in range(1, far):
            best = jnp.maximum(best, d * need[d if way == 0 else z_n - d])
        reach.append(best)
    same = jnp.right_shift(sub, pshift) == jnp.right_shift(lane, pshift)
    same_f = jnp.where(same, 1.0, 0.0)

    def numbers(depth):
        rows = [jnp.where(reach[way] >= d, 1.0, 0.0) for way in (0, 1) for d in range(1, depth + 1)]
        stacked = jnp.concatenate(rows + [rows[0]] * (8 - len(rows)), axis=0)
        total = jnp.dot(stacked, same_f, preferred_element_type=F32)
        return [[None] + [total[way * depth + d:way * depth + d + 1] for d in range(depth)] for way in (0, 1)]

    def from_back(way, row, back):
        step = per * (back % z_n)
        step = step if way == 0 else (LANES - step) % LANES
        return row if step == 0 else pltpu.roll(jnp.broadcast_to(row, (8, LANES)), step, 1)[0:1]

    beyond = []
    for way, number in enumerate(numbers(far - 1)):
        load = sum(from_back(way, number[d], d - 1) for d in range(1, far))
        beyond.append(sum(jnp.where(reach[way] <= e, from_back(way, load, -e), 0.0) for e in range(far)))
    odd = jnp.bitwise_and(lane_row, 1).astype(F32)
    lead = beyond[1] - beyond[0] + 0.5 - odd
    reach = [
        jnp.where(lead > 0, jnp.maximum(reach[0], far * need[far]), reach[0]),
        jnp.where(lead > 0, reach[1], jnp.maximum(reach[1], far * need[far])),
    ]

    longest = jnp.zeros((1, 1), F32)
    places, puts = [], []
    for way, (reach_col, number) in enumerate(zip(columns(reach), numbers(far))):
        ahead = jnp.logical_or(reach_col > reach[way], jnp.logical_and(reach_col == reach[way], sub < lane))
        rank = hits(jnp.logical_and(same, ahead))

        start = [None, jnp.zeros((1, LANES), F32)]
        for d in range(2, far + 1):
            before = from_back(way, number[d - 1], d - 2)
            start.append(jnp.maximum(start[d - 1] + before, from_back(way, start[d - 1], 1) + GAP))
        length = start[far] + from_back(way, number[far], far - 1)
        longest = jnp.maximum(longest, jnp.max(length, axis=1, keepdims=True))

        def of(row, shard):
            return jnp.max(jnp.where(src_row == shard, row, 0.0), axis=1, keepdims=True)

        back = lax.rem(z + (z_n - 1 if way == 0 else 1), z_n)
        away = jnp.bitwise_and(z - src_row + z_n, z_n - 1)
        if way == 1:
            away = jnp.bitwise_and(z_n - away, z_n - 1)
        got, put = rank, rank
        for d in range(2, far + 1):
            got = got + jnp.where(away == d, of(start[d], back), 0.0)
            put = put + jnp.where(away == d - 1, of(start[d], z), 0.0)
        place = jnp.where(away == 0, blk_row, per + TOP * way + got)
        away_f = away.astype(F32)
        put = jnp.where(jnp.logical_and(away_f < far, reach[way] > away_f), put, -1.0)
        puts.append(put)
        places.append(place)

    away = jnp.bitwise_and(z - src_row + z_n, z_n - 1)
    opposite = jnp.where(reach[0] == float(far), places[0], places[1])
    place = jnp.where(away < far, places[0], jnp.where(away == far, opposite, places[1]))
    put_cols = columns(puts + places + [place])
    orders = [hits(put_cols[way] == lane_f, put_cols[2 + way]) for way in (0, 1)]
    at_slot = hits(sub == mine[0:1], put_cols[4])

    plan[...] = jnp.zeros_like(plan)
    plan[0:1, :] = orders[0].astype(I32)
    plan[1:2, :] = orders[1].astype(I32)
    plan[2:3, :] = at_slot.astype(I32)
    plan[3:4, 0:slots] = m * fb + narrow_at
    top = jnp.max(longest)
    level[0] = sum(jnp.where(top > room, 1, 0) for room in SIZES[:-1])
    for swap in swaps:
        swap.wait_send()
    out.wait()


def kernel(dims, turned, gate_hbm, up_hbm, grad_hbm, plan, counts, out_ref, gate_in, up_in, grad_in,
           f_buf, acc, load_sem, own_sem, ring_send, ring_recv, pair_send, pair_recv, sum_send, sum_recv, *bufs):
    room, dp_n, z_n, tokens, per, fb, slots = dims
    waves = len(ROWS)
    held = bufs[0:waves]
    stage = bufs[waves:2 * waves]
    came = bufs[2 * waves:3 * waves]
    p_out = bufs[3 * waves:4 * waves]
    p_own = bufs[4 * waves:5 * waves]
    p_in = bufs[5 * waves:6 * waves]
    s_buf = bufs[6 * waves:7 * waves]
    r_buf = bufs[7 * waves:8 * waves]
    chips = dp_n // 2
    half = slots // 2

    dp = lax.axis_index("dp")
    z = lax.axis_index("tensor")
    core = lax.rem(dp, 2)
    chip = lax.div(dp, 2)
    sibling = dp + 1 - 2 * core
    right, left = lax.rem(z + 1, z_n), lax.rem(z + z_n - 1, z_n)
    starts = [sum(ROWS[:w]) for w in range(waves)]

    own = [
        pltpu.make_async_copy(turned.at[:, pl.ds(starts[w], ROWS[w])], held[w].at[pl.ds(0, per)], own_sem.at[w])
        for w in range(waves)
    ]
    for load in own:
        load.start()
    loads = [
        pltpu.make_async_copy(src, dst, load_sem.at[i])
        for i, (src, dst) in enumerate(((gate_hbm, gate_in), (up_hbm, up_in), (grad_hbm, grad_in)))
    ]
    for load in loads:
        load.start()

    barrier = pltpu.get_barrier_semaphore()
    for to in (left, right):
        pl.semaphore_signal(barrier, inc=1, device_id=(dp, to), device_id_type=MESH)
    pl.semaphore_signal(barrier, inc=1, device_id=(sibling, z), device_id_type=MESH)

    def greet(o, _):
        pl.semaphore_signal(barrier, inc=1, device_id=(lax.rem(chip + o, chips) * 2 + core, z), device_id_type=MESH)
        return 0

    lax.fori_loop(1, chips, greet, 0)

    cuts = [(p, min(p + PART, room)) for p in range(0, room, PART)]
    parts = len(cuts)

    def message(w, way, q):
        first, last = cuts[q]
        cut = pl.ds(first, last - first)
        return pltpu.make_async_remote_copy(
            src_ref=stage[w].at[way, cut], dst_ref=came[w].at[way, cut],
            send_sem=ring_send.at[w, way], recv_sem=ring_recv.at[w, way, q],
            device_id=(dp, right if way == 0 else left), device_id_type=MESH)

    def fill(w, q):
        for p in range(*cuts[q]):
            for way in (0, 1):
                stage[w][way, p] = held[w][plan[way, p]]

    def send(w, q):
        fill(w, q)
        for way in (0, 1):
            message(w, way, q).start()

    def take(w, q):
        for way in (0, 1):
            message(w, way, q).wait_recv()

        first, last = cuts[q]
        for way in (0, 1):
            at = per + TOP * way
            held[w][at + first:at + last] = came[w][way, first:last]

    def back(f, _):
        cols = pl.ds(pl.multiple_of(f * BLK, BLK), BLK)
        g = gate_in[:, cols].astype(F32)
        u = up_in[:, cols].astype(F32)
        d = grad_in[:, cols].astype(F32)
        s = 1.0 / (1.0 + jnp.exp(-g))
        active = g * s
        f_buf[f] = (d * u * s * (1.0 + g * (1.0 - s))).astype(BF16)
        f_buf[fb + f] = (d * active).astype(BF16)
        f_buf[2 * fb + f] = (active * u).astype(BF16)
        return 0

    def products(w, dst, parity):
        def body(i, _):
            for j in range(GROUP):
                n = i * GROUP + j
                k = 2 * n + parity
                dst[n] = jnp.dot(held[w][plan[2, k]], f_buf[plan[3, k]], preferred_element_type=F32)
            return 0

        lax.fori_loop(0, half // GROUP, body, 0)

    def pair(w):
        return pltpu.make_async_remote_copy(
            src_ref=p_out[w], dst_ref=p_in[w], send_sem=pair_send.at[w], recv_sem=pair_recv.at[w],
            device_id=(sibling, z), device_id_type=MESH)

    def spread(w):
        pair(w).wait_recv()

        def add(n, _):
            s_buf[w][n] = (p_own[w][n] + p_in[w][n]).astype(BF16)
            return 0

        lax.fori_loop(0, chips, add, 0)

        def post(o, _):
            to = lax.rem(chip + o, chips)
            pltpu.make_async_remote_copy(
                src_ref=s_buf[w].at[to], dst_ref=r_buf[w].at[o - 1], send_sem=sum_send.at[w], recv_sem=sum_recv.at[w],
                device_id=(to * 2 + core, z), device_id_type=MESH).start()
            return 0

        lax.fori_loop(1, chips, post, 0)

    def all_sums(w):
        return pltpu.make_async_remote_copy(
            src_ref=s_buf[w].at[pl.ds(0, chips - 1)], dst_ref=r_buf[w], send_sem=sum_send.at[w], recv_sem=sum_recv.at[w],
            device_id=(sibling, z), device_id_type=MESH)

    def collect(w):
        all_sums(w).wait_recv()
        total = p_own[w][chip] + p_in[w][chip]
        for o in range(chips - 1):
            total = total + r_buf[w][o].astype(F32)
        acc[pl.ds(starts[w], ROWS[w])] = total

    def make_sib(w):
        products(w, p_out[w], 1 - core)
        pair(w).start()

    def make_own(w):
        products(w, p_own[w], core)

    events = sorted((BEGIN[w] * parts + q, w, q) for w in range(waves) for q in range(parts + LAG))
    todo = []
    for i, (_, w, q) in enumerate(events):
        if q >= LAG:
            take(w, q - LAG)
        if q == 0:
            own[w].wait()
        if q < parts:
            if i == 0:
                fill(w, q)
                pl.semaphore_wait(barrier, 3 + chips - 1)
                for way in (0, 1):
                    message(w, way, q).start()
            else:
                send(w, q)
        if i == LAG - 1:
            for load in loads:
                load.wait()
            lax.fori_loop(0, fb, back, 0)
        if q == parts + LAG - 1:
            todo += [(i, make_sib, w), (i + 1, make_own, w), (i + 5, spread, w)]
        while todo and todo[0][0] <= i:
            _, task, which = todo.pop(0)
            task(which)
        todo.sort(key=lambda entry: entry[0])
    for _, task, which in todo:
        task(which)
    for w in range(waves - 1):
        collect(w)
    for w in range(waves):
        for way in (0, 1):
            pltpu.make_async_remote_copy(
                src_ref=stage[w].at[way], dst_ref=came[w].at[way], send_sem=ring_send.at[w, way], recv_sem=ring_recv.at[w, way, 0],
                device_id=(dp, right), device_id_type=MESH).wait_send()
        pair(w).wait_send()
    collect(waves - 1)

    value = acc[...]
    down = plan[3, dp] >= 2 * fb
    value = jnp.where(down, value.T, value)
    scale = float(tokens * dp_n) ** (-0.5)
    live = (dp < counts[0]).astype(F32)
    out_ref[0, 0] = value * scale * live

    for w in range(waves):
        all_sums(w).wait_send()


def solution(mesh):
    dp_n, z_n = mesh.shape["dp"], mesh.shape["tensor"]
    vmem = pltpu.VMEM
    dma = pltpu.SemaphoreType.DMA
    hbm = pl.BlockSpec(memory_space=pl.ANY)
    smem = pl.BlockSpec(memory_space=pltpu.SMEM)
    whole = pl.BlockSpec(memory_space=pltpu.VMEM)

    def params(number):
        return pltpu.CompilerParams(collective_id=number, has_side_effects=True, vmem_limit_bytes=62 * 1024 * 1024)

    def per_device(activations, out_grad, gate_pre, up_pre, hidden_grad, kept_blocks, kept_counts):
        tokens, wide = activations.shape
        narrow = gate_pre.shape[1]
        slots = kept_blocks.shape[2]
        chips, half = dp_n // 2, slots // 2
        xb, fb = wide // BLK, narrow // BLK
        per = 2 * xb
        waves = len(ROWS)
        turned, plan, level = pl.pallas_call(
            functools.partial(plan_kernel, (z_n, xb, fb, slots)),
            out_shape=(
                jax.ShapeDtypeStruct((per, BLK, tokens), BF16),
                jax.ShapeDtypeStruct((8, LANES), I32),
                jax.ShapeDtypeStruct((1,), I32),
            ),
            in_specs=[hbm, hbm, whole, smem],
            out_specs=(hbm, whole, smem),
            scratch_shapes=[
                vmem((tokens, wide), BF16),
                vmem((tokens, wide), BF16),
                vmem((per, BLK, tokens), BF16),
                vmem((8, LANES), I32),
                vmem((z_n, 8, LANES), I32),
                dma((2,)),
                dma,
                dma((z_n - 1,)),
                dma((z_n - 1,)),
            ],
            compiler_params=params(0),
        )(activations, out_grad, kept_blocks.transpose(1, 0, 2), kept_counts)

        def run(number, room):
            parts = -(-room // PART)
            scratch = [vmem((tokens, narrow), BF16)] * 3 + [
                vmem((3 * fb, tokens, BLK), BF16),
                vmem((BLK, BLK), F32),
                dma((3,)),
                dma((waves,)),
                dma((waves, 2)),
                dma((waves, 2, parts)),
                dma((waves,)),
                dma((waves,)),
                dma((waves,)),
                dma((waves,)),
            ]
            scratch += [vmem((per + 2 * TOP, r, tokens), BF16) for r in ROWS]
            scratch += [vmem((2, room, r, tokens), BF16) for r in ROWS]
            scratch += [vmem((2, room, r, tokens), BF16) for r in ROWS]
            scratch += [vmem((half, r, BLK), F32) for r in ROWS]
            scratch += [vmem((half, r, BLK), F32) for r in ROWS]
            scratch += [vmem((half, r, BLK), F32) for r in ROWS]
            scratch += [vmem((chips, r, BLK), BF16) for r in ROWS]
            scratch += [vmem((chips - 1, r, BLK), BF16) for r in ROWS]
            return pl.pallas_call(
                functools.partial(kernel, (room, dp_n, z_n, tokens, per, fb, slots)),
                out_shape=jax.ShapeDtypeStruct((1, 1, BLK, BLK), F32),
                in_specs=[hbm] * 4 + [smem] * 2,
                out_specs=whole,
                scratch_shapes=scratch,
                compiler_params=params(number),
            )

        runs = [run(i + 1, room) for i, room in enumerate(SIZES)]
        return lax.switch(level[0], runs, turned, gate_pre, up_pre, hidden_grad, plan, kept_counts)

    return jax.shard_map(
        per_device,
        mesh=mesh,
        in_specs=(P("dp", "tensor"),) * 5 + (P("tensor", None, None), P("tensor")),
        out_specs=P("dp", "tensor", None, None),
        check_vma=False,
    )
```
